32 devices in a mesh: pipe: 4 (over z), expert: 8 (over y, x, core).
Axes of the slice: x: 2, y: 2, z: 4, core: 2. Of those that a mesh axis runs over, the one named last changes fastest.
Arguments:
- tokens_up: bfloat16 [2, 256, 3584], P(None, 'expert'), may hold values from -6 to 6
- tokens_down: bfloat16 [2, 256, 3584], P(None, 'expert'), may hold values from -6 to 6
- norm_gain: float32 [4, 3584], P('pipe'), may hold values from 0.1 to 1.9
- w_gate: bfloat16 [4, 3584, 8192], P('pipe', None, 'expert'), may hold values from -0.09375 to 0.09375
- w_up: bfloat16 [4, 3584, 8192], P('pipe', None, 'expert'), may hold values from -0.09375 to 0.09375
- w_down: bfloat16 [4, 8192, 3584], P('pipe', 'expert'), may hold values from -0.1875 to 0.1875
- route_up: int32 [4, 2, 256, 2], P('pipe', None, 'expert'), may hold values from 0 to 7, all different within a row; in each aligned block of 32 rows (0 to 31, 32 to 63, ..., all dimensions but the last counted through in order) at most 16 rows name the same one
- route_down: int32 [4, 2, 256, 2], P('pipe', None, 'expert'), may hold values from 0 to 7, all different within a row; in each aligned block of 32 rows (0 to 31, 32 to 63, ..., all dimensions but the last counted through in order) at most 16 rows name the same one
- gate_up: float32 [4, 2, 256, 2], P('pipe', None, 'expert'), may hold values from 0.1 to 1
- gate_down: float32 [4, 2, 256, 2], P('pipe', None, 'expert'), may hold values from 0.1 to 1
Outputs:
- acts_up: bfloat16 [4, 2, 256, 3584], P('pipe', None, 'expert')
- acts_down: bfloat16 [4, 2, 256, 3584], P('pipe', None, 'expert')
The draws below stay inside these ranges and needn't reach their ends.
Inputs may be any that keep to these rules, and one draw needn't show every extreme that they name: `route_up`: within the 32 rows of one device at one section and micro-batch (aligned blocks of 32 tokens), the 2 experts of a token differ, no expert is named more than 16 times, and in some block an expert is named exactly 16 times. `route_down`: within the 32 rows of one device at one section and micro-batch (aligned blocks of 32 tokens), the 2 experts of a token differ, no expert is named more than 16 times, and in some block an expert is named exactly 16 times.
All inputs are finite; a program needn't handle non-finite values.
Results may differ from the reference program's by a relative error of at most 0.0085.
Values may be sent and summed in bfloat16 or wider, within the bound.
No kernel may reach another device: no remote copies, remote signals or barrier semaphores. Data moves between devices by JAX's collectives and lax.ppermute only.
A program may use at most 128 MiB of HBM per device.

```python
import math
import jax
import jax.numpy as jnp
import numpy as np
from jax import lax

D = 3584
EXP_HID = 1024
TOP = 2
MICRO = 2
TOK_DEV = 32
SEGMENTS = 4
EXPERTS = 8
MB_TOK = 256
CAP = 16
N_EXPERT = 8


def levels(own_key, shape, shards, least, high):
    def one(axis_at, parts):
        draws = jax.random.uniform(jax.random.fold_in(jax.random.fold_in(own_key, 6), axis_at), (parts,), jnp.float32, least / len(shards), high / len(shards))
        return jnp.repeat(jnp.exp(draws), shape[axis_at] // parts).reshape((-1,) + (1,) * (len(shape) - axis_at - 1))

    gain = one(*shards[0])
    for cut in shards[1:]:
        gain = gain * one(*cut)
    return gain


def shared_out(own_key, own, number, rows, count, top, bound, lean):
    ranking = jax.random.permutation(own_key, count)
    packed, common = portions_of(count, rows * top, bound, lean, True), portions_of(count, rows * top, bound, lean, False)
    places = jnp.arange(count)

    def named(sizes, rotation):
        used = int((sizes > 0).sum())
        fixed = max(1, used // 4)
        moved = fixed + (places - fixed + rotation * (used - fixed)) % max(1, count - fixed)
        return jnp.zeros((count,), jnp.int32).at[ranking[jnp.where(places < fixed, places, moved)]].set(jnp.asarray(sizes, jnp.int32))

    sizes = jnp.where(number % 4 == 0, named(packed, number // 4), named(common, number - number // 4 - 1))
    mixed = jax.random.permutation(jax.random.fold_in(own, 3), count)
    source_of, receiver = mixed[0:count // 2 * 2:2], mixed[1:count // 2 * 2:2]
    room = jnp.minimum(sizes[source_of] - 1, bound - sizes[receiver]) // 2
    room = jnp.where((source_of == ranking[0]) | (receiver == ranking[0]) | (sizes[receiver] == 0), 0, jnp.maximum(room, 0))
    moved = jax.random.randint(jax.random.fold_in(own, 4), (count // 2,), 0, 1 << 20) % (room + 1)
    sizes = sizes.at[source_of].add(-moved).at[receiver].add(moved)
    members = jnp.searchsorted(jnp.cumsum(sizes), jnp.arange(rows * top), side="right").astype(jnp.int32)
    table = members.reshape(top, rows).T
    table = table[jax.random.permutation(jax.random.fold_in(own, 1), rows)]
    rotation = jax.random.randint(jax.random.fold_in(own, 2), (rows, 1), 0, top)
    return jnp.take_along_axis(table, (jnp.arange(top)[None, :] + rotation) % top, axis=1)


def portions_of(count, total, bound, skew, full):
    portions = [(1 << 20) // math.isqrt(grade ** skew) + 1 for grade in range(1, count + 1)]
    largest = bound if full else min(bound, max(-(-total // count), total * portions[0] // sum(portions)))
    least = 1 if total - largest >= count - 1 else 0
    counts, rest = [largest] + [least] * (count - 1), total - largest - least * (count - 1)
    while rest > 0:
        free = [i for i in range(1, count) if counts[i] < largest] or [i for i in range(1, count) if counts[i] < bound]
        whole, remaining = sum([portions[i] for i in free]), rest
        for i in free:
            more = min(bound - counts[i], max(1, remaining * portions[i] // whole), rest)
            counts[i] = counts[i] + more
            rest = rest - more
    return np.array(counts)


def noise(stream_key, dims, spread, most, pieces=(), kind=jnp.bfloat16):
    drawn = jax.random.normal(stream_key, dims, jnp.float32) * spread
    if len(pieces) > 0:
        drawn = levels(stream_key, dims, pieces, -0.22, 0.18) * drawn
    return jnp.clip(drawn, min=-most, max=most).astype(kind)


def setup_inputs(seed: int = 0) -> dict:
    keys = jax.random.split(jax.random.key(seed), 11)
    tokens_up = noise(keys[0], (MICRO, MB_TOK, D), 1.0, 6.0, ((1, 8),))
    tokens_down = noise(keys[1], (MICRO, MB_TOK, D), 1.0, 6.0, ((1, 8),))
    norm_gain = jnp.clip(1.0 + 0.18 * jax.random.normal(keys[2], (SEGMENTS, D), jnp.float32), 0.1, 1.9)
    w_gate = noise(keys[3], (SEGMENTS, D, EXPERTS * EXP_HID), D ** -0.5, 0.09375, ((0, 4), (2, 8)))
    w_up = noise(keys[4], (SEGMENTS, D, EXPERTS * EXP_HID), D ** -0.5, 0.09375, ((0, 4), (2, 8)))
    w_down = noise(keys[5], (SEGMENTS, EXPERTS * EXP_HID, D), EXP_HID ** -0.5, 0.1875, ((0, 4), (1, 8)))
    route_up_keys = jax.random.split(jax.random.fold_in(keys[6], 1), SEGMENTS * MICRO * MB_TOK // TOK_DEV)
    route_up_turns = jax.random.permutation(jax.random.fold_in(keys[6], 3), SEGMENTS * MICRO * MB_TOK // TOK_DEV)
    route_up = jax.vmap(lambda own, number: shared_out(jax.random.fold_in(keys[6], 2), own, number, TOK_DEV, EXPERTS, TOP, CAP, 2))(route_up_keys, route_up_turns).reshape((SEGMENTS, MICRO, MB_TOK, TOP))
    route_down_keys = jax.random.split(jax.random.fold_in(keys[7], 1), SEGMENTS * MICRO * MB_TOK // TOK_DEV)
    route_down_turns = jax.random.permutation(jax.random.fold_in(keys[7], 3), SEGMENTS * MICRO * MB_TOK // TOK_DEV)
    route_down = jax.vmap(lambda own, number: shared_out(jax.random.fold_in(keys[7], 2), own, number, TOK_DEV, EXPERTS, TOP, CAP, 2))(route_down_keys, route_down_turns).reshape((SEGMENTS, MICRO, MB_TOK, TOP))
    gate_up = jnp.clip(jnp.exp(math.log(1.0) - 2.3025851 * jax.random.uniform(keys[8], (SEGMENTS, MICRO, MB_TOK, TOP), jnp.float32) ** levels(keys[8], (SEGMENTS, MICRO, MB_TOK, TOP), ((0, 4), (2, 8)), -0.2, 0.2)), 0.1, 1.0)
    gate_down = jnp.clip(jnp.exp(math.log(1.0) - 2.3025851 * jax.random.uniform(keys[9], (SEGMENTS, MICRO, MB_TOK, TOP), jnp.float32) ** levels(keys[9], (SEGMENTS, MICRO, MB_TOK, TOP), ((0, 4), (2, 8)), -0.2, 0.2)), 0.1, 1.0)
    return dict(tokens_up=tokens_up, tokens_down=tokens_down, norm_gain=norm_gain, w_gate=w_gate, w_up=w_up, w_down=w_down, route_up=route_up, route_down=route_down, gate_up=gate_up, gate_down=gate_down)


def normalize(hidden_in, norm_scale):
    values = hidden_in.astype(jnp.float32)
    meansq = lax.optimization_barrier(jnp.mean(values * values, axis=-1, keepdims=True))
    normed = (values * lax.rsqrt(meansq + 1e-06) * norm_scale.astype(jnp.float32)).astype(jnp.bfloat16)
    return (values, normed)

def expert_rows(inputs, gate_cols, up_cols, down_rows):
    first_proj = jnp.dot(inputs, gate_cols, preferred_element_type=jnp.float32)
    second_proj = jnp.dot(inputs, up_cols, preferred_element_type=jnp.float32)
    hidden = (jax.nn.silu(first_proj) * second_proj).astype(jnp.bfloat16)
    return jnp.dot(hidden, down_rows, preferred_element_type=jnp.float32).astype(jnp.bfloat16)

def apply_section(section, hidden_in, norm_gain, w_gate, w_up, w_down, route_ids, gate_vals):
    values, normed = normalize(hidden_in, norm_gain[section])
    flat_ids = route_ids.reshape(-1).astype(jnp.int32)
    flat_gates = gate_vals.reshape(-1).astype(jnp.float32)
    limit = N_EXPERT * CAP
    positions = jnp.arange(limit, dtype=jnp.int32)
    gate_all = w_gate[section]
    up_all = w_up[section]
    down_all = w_down[section]

    def per_expert(total, expert_no):
        hits = flat_ids == expert_no
        live_count = jnp.sum(hits.astype(jnp.int32))
        found = jnp.nonzero(hits, size=limit, fill_value=0)[0].astype(jnp.int32)
        token_no = found // TOP
        inputs = jnp.take(normed, token_no, axis=0)
        start = (expert_no * EXP_HID).astype(jnp.int32)
        gate_cols = lax.dynamic_slice_in_dim(gate_all, start, EXP_HID, 1)
        up_cols = lax.dynamic_slice_in_dim(up_all, start, EXP_HID, 1)
        down_rows = lax.dynamic_slice_in_dim(down_all, start, EXP_HID, 0)
        outputs = expert_rows(inputs, gate_cols, up_cols, down_rows).astype(jnp.float32)
        weight_col = jnp.where(positions < live_count, jnp.take(flat_gates, found), jnp.zeros((), jnp.float32))
        return (total.at[token_no].add(weight_col[:, None] * outputs), None)
    total, unused = lax.scan(per_expert, values, jnp.arange(EXPERTS, dtype=jnp.int32))
    return total.astype(jnp.bfloat16)

def reference(tokens_up, tokens_down, norm_gain, w_gate, w_up, w_down, route_up, route_down, gate_up, gate_down):
    rows_up = [[] for section in range(SEGMENTS)]
    rows_down = [[] for section in range(SEGMENTS)]
    for micro_no in range(MICRO):
        current = tokens_up[micro_no]
        for section in range(SEGMENTS):
            current = apply_section(section, current, norm_gain, w_gate, w_up, w_down, route_up[section, micro_no], gate_up[section, micro_no])
            rows_up[section].append(current)
        current = tokens_down[micro_no]
        for section in reversed(range(SEGMENTS)):
            current = apply_section(section, current, norm_gain, w_gate, w_up, w_down, route_down[section, micro_no], gate_down[section, micro_no])
            rows_down[section].append(current)
    acts_up = jnp.stack([jnp.stack(rows_up[section]) for section in range(SEGMENTS)])
    acts_down = jnp.stack([jnp.stack(rows_down[section]) for section in range(SEGMENTS)])
    return (acts_up, acts_down)
```

```python
import functools

import jax
import jax.numpy as jnp
from jax import lax
from jax.experimental import pallas as pl
from jax.experimental.pallas import tpu as pltpu
from jax.sharding import PartitionSpec as P

AXES = ("pipe", "expert")
COLS = 512
HIDS = 256


def expert_kernel(
    rows, near_ref, far_ref, pick_ref, put_ref, weight_ref, gain_ref, gate_ref, up_ref, down_ref,
    mine_ref, other_ref, picked, hidden,
):
    width = near_ref.shape[1]
    cols = min(COLS, width)
    hids = min(HIDS, gate_ref.shape[1])
    slots = pick_ref.shape[0]

    def gather(step, total):
        at = pl.ds(pl.multiple_of(step * cols, cols), cols)
        block = jnp.dot(pick_ref[:, :rows], near_ref[:, at], preferred_element_type=jnp.float32)
        block += jnp.dot(pick_ref[:, rows:], far_ref[:, at], preferred_element_type=jnp.float32)
        picked[:, at] = block.astype(jnp.bfloat16)
        return total + jnp.sum(block * block, axis=1, keepdims=True)

    total = lax.fori_loop(0, width // cols, gather, jnp.zeros((slots, 1), jnp.float32))
    scale = lax.rsqrt(total / width + 1e-06)

    def norm(step, carry):
        at = pl.ds(pl.multiple_of(step * cols, cols), cols)
        block = picked[:, at].astype(jnp.float32) * scale * gain_ref[:, at]
        picked[:, at] = block.astype(jnp.bfloat16)
        return carry

    lax.fori_loop(0, width // cols, norm, 0)

    def project(step, carry):
        at = pl.ds(pl.multiple_of(step * hids, hids), hids)
        first = jnp.dot(picked[...], gate_ref[:, at], preferred_element_type=jnp.float32)
        second = jnp.dot(picked[...], up_ref[:, at], preferred_element_type=jnp.float32)
        hidden[:, at] = (first / (1.0 + jnp.exp(-first)) * second).astype(jnp.bfloat16)
        return carry

    lax.fori_loop(0, gate_ref.shape[1] // hids, project, 0)

    def scatter(step, carry):
        at = pl.ds(pl.multiple_of(step * cols, cols), cols)
        block = jnp.dot(hidden[...], down_ref[:, at], preferred_element_type=jnp.float32)
        block = jnp.dot(put_ref[...], block.astype(jnp.bfloat16), preferred_element_type=jnp.float32)
        block = (block * weight_ref[...]).astype(jnp.bfloat16)
        mine_ref[:, at] = block[:rows]
        other_ref[:, at] = block[rows:]
        return carry

    lax.fori_loop(0, width // cols, scatter, 0)


def expert_call(near, far, pick, put, weight, gain, gate_cols, up_cols, down_rows):
    rows, width = near.shape
    slots, hid = pick.shape[0], gate_cols.shape[1]
    out = jax.ShapeDtypeStruct((rows, width), jnp.bfloat16)
    whole = pl.BlockSpec(memory_space=pltpu.VMEM)
    return pl.pallas_call(
        functools.partial(expert_kernel, rows),
        out_shape=(out, out),
        in_specs=[whole] * 9,
        out_specs=(whole, whole),
        scratch_shapes=[
            pltpu.VMEM((slots, width), jnp.bfloat16),
            pltpu.VMEM((slots, hid), jnp.bfloat16),
        ],
        compiler_params=pltpu.CompilerParams(vmem_limit_bytes=56 * 2**20),
        cost_estimate=pl.CostEstimate(
            flops=6 * slots * width * hid, bytes_accessed=6 * width * hid, transcendentals=slots * hid
        ),
    )(near, far, pick, put, weight, gain, gate_cols, up_cols, down_rows)


def on_device(
    tokens_up, tokens_down, norm_gain, w_gate, w_up, w_down, route_up, route_down, gate_up, gate_down
):
    plane, me = lax.axis_index("pipe"), lax.axis_index("expert")
    planes, experts = lax.axis_size("pipe"), lax.axis_size("expert")
    micros, tokens, width = tokens_up.shape
    top = route_up.shape[3]
    capacity = min(tokens, 2 * tokens * top // experts)
    low = plane < planes // 2
    layer = (norm_gain, w_gate[0], w_up[0], w_down[0])
    masks = list(range(0, experts, 2)) + list(range(1, experts, 2))
    half = experts // 2

    def exchange(block, active, mask):
        pairs = [(p * experts + i, p * experts + (i ^ mask)) for p in active for i in range(experts)]
        return lax.ppermute(block, AXES, pairs)

    def ordered(up, down):
        return [jnp.where(low, up, down), jnp.where(low, down, up)]

    tables = jnp.stack(
        [
            jnp.stack(ordered(route_up[0].astype(jnp.float32), route_down[0].astype(jnp.float32))),
            jnp.stack(ordered(gate_up[0], gate_down[0])),
        ]
    )
    tables = lax.all_gather(tables, "expert", axis=0)
    source = (me ^ jnp.array(masks, jnp.int32))[:, None] == jnp.arange(experts)
    tables = jnp.sum(jnp.where(source.reshape(source.shape + (1,) * 5), tables, 0.0), axis=1)
    hits = (tables[:, 0] == me.astype(jnp.float32)).astype(jnp.float32)
    weights = jnp.sum(hits * tables[:, 1], axis=-1)
    hits = jnp.sum(hits, axis=-1)
    before = (jnp.arange(tokens)[:, None] < jnp.arange(tokens)[None, :]).astype(jnp.float32)
    places = jnp.einsum("dsmt,tu->dsmu", hits, before)
    places += capacity * jnp.arange(experts, dtype=jnp.float32)[:, None, None, None]
    places = jnp.where(hits > 0, places, -1.0)
    places = places.transpose(1, 2, 0, 3).reshape(2, micros, experts * tokens)
    weights = weights.transpose(1, 2, 0, 3).reshape(2, micros, experts * tokens, 1)
    slots = jnp.arange(experts * capacity, dtype=jnp.float32)
    pick = (places[:, :, None, :] == slots[:, None]).astype(jnp.bfloat16)
    put = (places[:, :, :, None] == slots).astype(jnp.bfloat16)

    entering = [jnp.where(low, tokens_up[m], tokens_down[m]) for m in range(micros)]
    results = []
    for tick in range(planes):
        stream = 0 if tick < planes // 2 else 1
        active = (tick, planes - 1 - tick)
        leaving = []
        for m in range(micros):
            own = entering[m]
            near = jnp.concatenate([own] + [exchange(own, active, mask) for mask in masks[1:half]])
            far = exchange(near, active, 1)
            mine, other = expert_call(
                near, far, pick[stream, m], put[stream, m], weights[stream, m], *layer
            )
            other = exchange(other, active, 1)
            sums = mine.astype(jnp.float32) + other.astype(jnp.float32)
            total = own.astype(jnp.float32) + sums[:tokens]
            parts = sums.astype(jnp.bfloat16)
            for j in range(1, half):
                part = parts[j * tokens : (j + 1) * tokens]
                total += exchange(part, active, masks[j]).astype(jnp.float32)
            leaving.append(total.astype(jnp.bfloat16))
        results.append(leaving)
        if tick + 1 < planes:
            pairs = [(tick, tick + 1), (planes - 1 - tick, planes - 2 - tick)]
            entering = [lax.ppermute(block, "pipe", pairs) for block in leaving]

    first = jnp.minimum(plane, planes - 1 - plane)
    acts = []
    for ticks, at in (
        (range(planes // 2), first),
        (range(planes // 2, planes), planes - 1 - first),
    ):
        chosen = jnp.stack(results[ticks[0]])
        for tick in ticks[1:]:
            chosen = jnp.where(at == tick, jnp.stack(results[tick]), chosen)
        acts.append(chosen)
    return (jnp.where(low, acts[0], acts[1])[None], jnp.where(low, acts[1], acts[0])[None])


def solution(mesh):
    in_specs = (
        P(None, "expert", None),
        P(None, "expert", None),
        P("pipe", None),
        P("pipe", None, "expert"),
        P("pipe", None, "expert"),
        P("pipe", "expert", None),
        P("pipe", None, "expert", None),
        P("pipe", None, "expert", None),
        P("pipe", None, "expert", None),
        P("pipe", None, "expert", None),
    )
    out_specs = (P("pipe", None, "expert", None), P("pipe", None, "expert", None))
    return jax.shard_map(
        on_device, mesh=mesh, in_specs=in_specs, out_specs=out_specs, check_vma=False
    )
```

```python
import functools

import jax
import jax.numpy as jnp
from jax import lax
from jax.experimental import pallas as pl
from jax.experimental.pallas import tpu as pltpu
from jax.sharding import PartitionSpec as P

AXES = ("pipe", "expert")
BLOCKS = 2
HIDS = 256


def spans(size, step):
    return [slice(at, at + step) for at in range(0, size, step)]


def expert_kernel(count, *refs):
    blocks, refs = refs[:count], refs[count:]
    pick_ref, put_ref, weight_ref, gain_ref, gate_hbm, up_hbm, down_hbm = refs[:7]
    outs, refs = refs[7 : 7 + count], refs[7 + count :]
    rows_ref, picked, hidden, gate_ref, up_ref, down_ref, sems = refs
    tokens = blocks[0].shape[0]
    width, hid = gate_ref.shape
    wides, hids = spans(width, width // BLOCKS), spans(hid, HIDS)

    copies = []
    for source, target, at in (
        [(a, b, at) for at in hids for a, b in ((gate_hbm, gate_ref), (up_hbm, up_ref))]
        + [(down_hbm, down_ref, at) for at in wides]
    ):
        copies.append(
            pltpu.make_async_copy(source.at[:, at], target.at[:, at], sems.at[len(copies)])
        )
        copies[-1].start()
    arriving = iter(copies)

    for i, ref in enumerate(blocks):
        rows_ref[i * tokens : (i + 1) * tokens] = ref[...]
    total = 0.0
    for at in wides:
        block = jnp.dot(pick_ref[...], rows_ref[:, at], preferred_element_type=jnp.float32)
        picked[:, at] = block.astype(jnp.bfloat16)
        total += jnp.sum(block * block, axis=1, keepdims=True)
    scale = lax.rsqrt(total / width + 1e-06)
    for at in wides:
        block = picked[:, at].astype(jnp.float32) * scale * gain_ref[:, at]
        picked[:, at] = block.astype(jnp.bfloat16)
    for at in hids:
        next(arriving).wait()
        first = jnp.dot(picked[...], gate_ref[:, at], preferred_element_type=jnp.float32)
        next(arriving).wait()
        second = jnp.dot(picked[...], up_ref[:, at], preferred_element_type=jnp.float32)
        hidden[:, at] = (first / (1.0 + jnp.exp(-first)) * second).astype(jnp.bfloat16)
    for at in wides:
        next(arriving).wait()
        block = jnp.dot(hidden[...], down_ref[:, at], preferred_element_type=jnp.float32)
        block = jnp.dot(put_ref[...], block.astype(jnp.bfloat16), preferred_element_type=jnp.float32)
        block = (block * weight_ref[...]).astype(jnp.bfloat16)
        for i, ref in enumerate(outs):
            ref[:, at] = block[i * tokens : (i + 1) * tokens]


def expert_call(blocks, pick, put, weight, gain, gate_cols, up_cols, down_rows):
    count, (tokens, width) = len(blocks), blocks[0].shape
    slots, hid = pick.shape[0], gate_cols.shape[1]
    whole = pl.BlockSpec(memory_space=pltpu.VMEM)
    return pl.pallas_call(
        functools.partial(expert_kernel, count),
        out_shape=[jax.ShapeDtypeStruct((tokens, width), jnp.bfloat16)] * count,
        in_specs=[whole] * (count + 4) + [pl.BlockSpec(memory_space=pltpu.HBM)] * 3,
        out_specs=[whole] * count,
        scratch_shapes=[
            pltpu.VMEM((count * tokens, width), jnp.bfloat16),
            pltpu.VMEM((slots, width), jnp.bfloat16),
            pltpu.VMEM((slots, hid), jnp.bfloat16),
            pltpu.VMEM((width, hid), jnp.bfloat16),
            pltpu.VMEM((width, hid), jnp.bfloat16),
            pltpu.VMEM((hid, width), jnp.bfloat16),
            pltpu.SemaphoreType.DMA((2 * (hid // HIDS) + BLOCKS,)),
        ],
        compiler_params=pltpu.CompilerParams(vmem_limit_bytes=(28 + count * tokens // 64) * 2**20),
        cost_estimate=pl.CostEstimate(
            flops=6 * slots * width * hid, bytes_accessed=6 * width * hid, transcendentals=slots * hid
        ),
    )(*blocks, pick, put, weight, gain, *(
        pltpu.with_memory_space_constraint(w, pltpu.HBM) for w in (gate_cols, up_cols, down_rows)
    ))


def after(values, earlier):
    return lax.optimization_barrier((values, earlier))


def on_device(
    tokens_up, tokens_down, norm_gain, w_gate, w_up, w_down, route_up, route_down, gate_up, gate_down
):
    plane, me = lax.axis_index("pipe"), lax.axis_index("expert")
    planes, experts = lax.axis_size("pipe"), lax.axis_size("expert")
    micros, tokens, width = tokens_up.shape
    top = route_up.shape[3]
    capacity = min(tokens, 2 * tokens * top // experts)
    low = plane < planes // 2
    layer = (norm_gain, w_gate[0], w_up[0], w_down[0])
    masks = list(range(0, experts, 2)) + list(range(1, experts, 2))
    half = experts // 2

    def exchange(block, active, mask):
        pairs = [(p * experts + i, p * experts + (i ^ mask)) for p in active for i in range(experts)]
        return lax.ppermute(block, AXES, pairs)

    def send_back(sums, active):
        return sums[:1] + [exchange(sums[j], active, masks[j]) for j in range(1, half)]

    def ordered(up, down):
        return [jnp.where(low, up, down), jnp.where(low, down, up)]

    tables = jnp.stack(
        [
            jnp.stack(ordered(route_up[0].astype(jnp.float32), route_down[0].astype(jnp.float32))),
            jnp.stack(ordered(gate_up[0], gate_down[0])),
        ]
    )
    tables = lax.all_gather(tables, "expert", axis=0)
    source = (me ^ jnp.array(masks, jnp.int32))[:, None] == jnp.arange(experts)
    tables = jnp.sum(jnp.where(source.reshape(source.shape + (1,) * 5), tables, 0.0), axis=1)
    hits = (tables[:, 0] == me.astype(jnp.float32)).astype(jnp.float32)
    weights = jnp.sum(hits * tables[:, 1], axis=-1)
    hits = jnp.sum(hits, axis=-1)
    before = (jnp.arange(tokens)[:, None] < jnp.arange(tokens)[None, :]).astype(jnp.float32)
    places = jnp.einsum("dsmt,tu->dsmu", hits, before)
    places += capacity * jnp.arange(experts, dtype=jnp.float32)[:, None, None, None]
    places = jnp.where(hits > 0, places, -1.0)
    places = places.transpose(1, 2, 0, 3).reshape(2, micros, experts * tokens)
    weights = weights.transpose(1, 2, 0, 3).reshape(2, micros, experts * tokens, 1)
    slots = jnp.arange(experts * capacity, dtype=jnp.float32)
    pick = (places[:, :, None, :] == slots[:, None]).astype(jnp.bfloat16)
    put = (places[:, :, :, None] == slots).astype(jnp.bfloat16)

    entering = [jnp.where(low, tokens_up[m], tokens_down[m]) for m in range(micros)]
    results = []
    for tick in range(planes):
        stream = 0 if tick < planes // 2 else 1
        active = (tick, planes - 1 - tick)
        near, sums, back = [], [], []
        for m in range(micros):
            own = entering[m]
            if m > 0:
                own, near[m - 1] = after(own, near[m - 1])
            arrived = [exchange(own, active, mask) for mask in masks[1:half]]
            if m > 0:
                arrived, sums[m - 1] = after(arrived, sums[m - 1])
                back.append(send_back(sums[m - 1], active))
            near.append([entering[m]] + arrived)
            far = [exchange(block, active, 1) for block in near[m]]
            outs = expert_call(
                near[m] + far, pick[stream, m], put[stream, m], weights[stream, m], *layer
            )
            if m > 0:
                back[m - 1], outs = after(back[m - 1], outs)
            total = [
                a.astype(jnp.float32) + exchange(b, active, 1).astype(jnp.float32)
                for a, b in zip(outs[:half], outs[half:])
            ]
            sums.append(total[:1] + [part.astype(jnp.bfloat16) for part in total[1:]])
        back.append(send_back(sums[-1], active))
        leaving = []
        for m in range(micros):
            total = entering[m].astype(jnp.float32)
            for part in back[m]:
                total += part.astype(jnp.float32)
            leaving.append(total.astype(jnp.bfloat16))
        results.append(leaving)
        if tick + 1 < planes:
            pairs = [(tick, tick + 1), (planes - 1 - tick, planes - 2 - tick)]
            entering = [lax.ppermute(block, "pipe", pairs) for block in leaving]

    first = jnp.minimum(plane, planes - 1 - plane)
    acts = []
    for ticks, at in (
        (range(planes // 2), first),
        (range(planes // 2, planes), planes - 1 - first),
    ):
        chosen = jnp.stack(results[ticks[0]])
        for tick in ticks[1:]:
            chosen = jnp.where(at == tick, jnp.stack(results[tick]), chosen)
        acts.append(chosen)
    return (jnp.where(low, acts[0], acts[1])[None], jnp.where(low, acts[1], acts[0])[None])


def solution(mesh):
    in_specs = (
        P(None, "expert", None),
        P(None, "expert", None),
        P("pipe", None),
        P("pipe", None, "expert"),
        P("pipe", None, "expert"),
        P("pipe", "expert", None),
        P("pipe", None, "expert", None),
        P("pipe", None, "expert", None),
        P("pipe", None, "expert", None),
        P("pipe", None, "expert", None),
    )
    out_specs = (P("pipe", None, "expert", None), P("pipe", None, "expert", None))
    return jax.shard_map(
        on_device, mesh=mesh, in_specs=in_specs, out_specs=out_specs, check_vma=False
    )
```

```python
import functools

import jax
import jax.numpy as jnp
from jax import lax
from jax.experimental import pallas as pl
from jax.experimental.pallas import tpu as pltpu
from jax.sharding import PartitionSpec as P

BLOCKS = 2
HIDS = 256


def spans(size, step):
    return [slice(at, at + step) for at in range(0, size, step)]


def expert_kernel(count, *refs):
    blocks, refs = refs[:count], refs[count:]
    pick_ref, put_ref, weight_ref, gain_ref, gate_hbm, up_hbm, down_hbm = refs[:7]
    outs, refs = refs[7 : 7 + count], refs[7 + count :]
    rows_ref, picked, hidden, gate_ref, up_ref, down_ref, sems = refs
    tokens = blocks[0].shape[0]
    width, hid = gate_ref.shape
    wides, hids = spans(width, width // BLOCKS), spans(hid, HIDS)

    copies = []
    for source, target, at in (
        [(a, b, at) for at in hids for a, b in ((gate_hbm, gate_ref), (up_hbm, up_ref))]
        + [(down_hbm, down_ref, at) for at in wides]
    ):
        copies.append(
            pltpu.make_async_copy(source.at[:, at], target.at[:, at], sems.at[len(copies)])
        )
        copies[-1].start()
    arriving = iter(copies)

    for i, ref in enumerate(blocks):
        rows_ref[i * tokens : (i + 1) * tokens] = ref[...]
    total = 0.0
    for at in wides:
        block = jnp.dot(pick_ref[...], rows_ref[:, at], preferred_element_type=jnp.float32)
        picked[:, at] = block.astype(jnp.bfloat16)
        total += jnp.sum(block * block, axis=1, keepdims=True)
    scale = lax.rsqrt(total / width + 1e-06)
    for at in wides:
        block = picked[:, at].astype(jnp.float32) * scale * gain_ref[:, at]
        picked[:, at] = block.astype(jnp.bfloat16)
    for at in hids:
        next(arriving).wait()
        first = jnp.dot(picked[...], gate_ref[:, at], preferred_element_type=jnp.float32)
        next(arriving).wait()
        second = jnp.dot(picked[...], up_ref[:, at], preferred_element_type=jnp.float32)
        hidden[:, at] = (first / (1.0 + jnp.exp(-first)) * second).astype(jnp.bfloat16)
    for at in wides:
        next(arriving).wait()
        block = jnp.dot(hidden[...], down_ref[:, at], preferred_element_type=jnp.float32)
        block = jnp.dot(put_ref[...], block.astype(jnp.bfloat16), preferred_element_type=jnp.float32)
        block = (block * weight_ref[...]).astype(jnp.bfloat16)
        for i, ref in enumerate(outs):
            ref[:, at] = block[i * tokens : (i + 1) * tokens]


def expert_call(blocks, pick, put, weight, gain, gate_cols, up_cols, down_rows):
    count, (tokens, width) = len(blocks), blocks[0].shape
    slots, hid = pick.shape[0], gate_cols.shape[1]
    whole = pl.BlockSpec(memory_space=pltpu.VMEM)
    return pl.pallas_call(
        functools.partial(expert_kernel, count),
        out_shape=[jax.ShapeDtypeStruct((tokens, width), jnp.bfloat16)] * count,
        in_specs=[whole] * (count + 4) + [pl.BlockSpec(memory_space=pltpu.HBM)] * 3,
        out_specs=[whole] * count,
        scratch_shapes=[
            pltpu.VMEM((count * tokens, width), jnp.bfloat16),
            pltpu.VMEM((slots, width), jnp.bfloat16),
            pltpu.VMEM((slots, hid), jnp.bfloat16),
            pltpu.VMEM((width, hid), jnp.bfloat16),
            pltpu.VMEM((width, hid), jnp.bfloat16),
            pltpu.VMEM((hid, width), jnp.bfloat16),
            pltpu.SemaphoreType.DMA((2 * (hid // HIDS) + BLOCKS,)),
        ],
        compiler_params=pltpu.CompilerParams(vmem_limit_bytes=(28 + count * tokens // 64) * 2**20),
        cost_estimate=pl.CostEstimate(
            flops=6 * slots * width * hid, bytes_accessed=6 * width * hid, transcendentals=slots * hid
        ),
    )(*blocks, pick, put, weight, gain, *(
        pltpu.with_memory_space_constraint(w, pltpu.HBM) for w in (gate_cols, up_cols, down_rows)
    ))


def after(values, earlier):
    return lax.optimization_barrier((values, earlier))


def on_device(
    tokens_up, tokens_down, norm_gain, w_gate, w_up, w_down, route_up, route_down, gate_up, gate_down
):
    plane, me = lax.axis_index("pipe"), lax.axis_index("expert")
    planes, experts = lax.axis_size("pipe"), lax.axis_size("expert")
    micros, tokens, width = tokens_up.shape
    top = route_up.shape[3]
    capacity = min(tokens, 2 * tokens * top // experts)
    low = plane < planes // 2
    layer = (norm_gain, w_gate[0], w_up[0], w_down[0])
    masks = list(range(0, experts, 2)) + list(range(1, experts, 2))
    half = experts // 2

    def exchange(block, mask):
        return lax.ppermute(block, "expert", [(i, i ^ mask) for i in range(experts)])

    def on_chip(outs):
        total = [
            a.astype(jnp.float32) + exchange(b, 1).astype(jnp.float32)
            for a, b in zip(outs[:half], outs[half:])
        ]
        return total[:1] + [part.astype(jnp.bfloat16) for part in total[1:]]

    def send_back(sums):
        return sums[:1] + [exchange(sums[j], masks[j]) for j in range(1, half)]

    def ordered(up, down):
        return [jnp.where(low, up, down), jnp.where(low, down, up)]

    tables = jnp.stack(
        [
            jnp.stack(ordered(route_up[0].astype(jnp.float32), route_down[0].astype(jnp.float32))),
            jnp.stack(ordered(gate_up[0], gate_down[0])),
        ]
    )
    tables = tables[None]
    for bit in range(experts.bit_length() - 1):
        tables = jnp.concatenate([tables, exchange(tables, 1 << bit)])
    tables = jnp.stack([tables[mask] for mask in masks])
    hits = (tables[:, 0] == me.astype(jnp.float32)).astype(jnp.float32)
    weights = jnp.sum(hits * tables[:, 1], axis=-1)
    hits = jnp.sum(hits, axis=-1)
    before = (jnp.arange(tokens)[:, None] < jnp.arange(tokens)[None, :]).astype(jnp.float32)
    places = jnp.einsum("dsmt,tu->dsmu", hits, before)
    places += capacity * jnp.arange(experts, dtype=jnp.float32)[:, None, None, None]
    places = jnp.where(hits > 0, places, -1.0)
    places = places.transpose(1, 2, 0, 3).reshape(2, micros, experts * tokens)
    weights = weights.transpose(1, 2, 0, 3).reshape(2, micros, experts * tokens, 1)
    slots = jnp.arange(experts * capacity, dtype=jnp.float32)
    pick = (places[:, :, None, :] == slots[:, None]).astype(jnp.bfloat16)
    put = (places[:, :, :, None] == slots).astype(jnp.bfloat16)

    tokens_up, tables_ready = after(tokens_up, tables)
    entering = [jnp.where(low, tokens_up[m], tokens_down[m]) for m in range(micros)]
    results = []
    for tick in range(planes):
        stream = 0 if tick < planes // 2 else 1
        near, sums, back = [], [], []
        for m in range(micros):
            own = entering[m]
            if m > 0:
                own, near[m - 1] = after(own, near[m - 1])
            arrived = [exchange(own, mask) for mask in masks[1:half]]
            if m > 0:
                arrived, outs = after(arrived, outs)
                sums.append(on_chip(outs))
                arrived, sums[m - 1] = after(arrived, sums[m - 1])
                back.append(send_back(sums[m - 1]))
            near.append([entering[m]] + arrived)
            far = [exchange(block, 1) for block in near[m]]
            outs = expert_call(
                near[m] + far, pick[stream, m], put[stream, m], weights[stream, m], *layer
            )
            if m > 0:
                back[m - 1], outs = after(back[m - 1], outs)
        sums.append(on_chip(outs))
        back.append(send_back(sums[-1]))
        leaving = []
        for m in range(micros):
            total = entering[m].astype(jnp.float32)
            for part in back[m]:
                total += part.astype(jnp.float32)
            leaving.append(total.astype(jnp.bfloat16))
        results.append(leaving)
        if tick + 1 < planes:
            ups = [(p, p + 1) for p in range(tick % 2, planes - 1, 2)]
            pairs = ups + [(b, a) for a, b in ups]
            entering = [lax.ppermute(block, "pipe", pairs) for block in leaving]

    first = jnp.minimum(plane, planes - 1 - plane)
    acts = []
    for ticks, at in (
        (range(planes // 2), first),
        (range(planes // 2, planes), planes - 1 - first),
    ):
        chosen = jnp.stack(results[ticks[0]])
        for tick in ticks[1:]:
            chosen = jnp.where(at == tick, jnp.stack(results[tick]), chosen)
        acts.append(chosen)
    return (jnp.where(low, acts[0], acts[1])[None], jnp.where(low, acts[1], acts[0])[None])


def solution(mesh):
    in_specs = (
        P(None, "expert", None),
        P(None, "expert", None),
        P("pipe", None),
        P("pipe", None, "expert"),
        P("pipe", None, "expert"),
        P("pipe", "expert", None),
        P("pipe", None, "expert", None),
        P("pipe", None, "expert", None),
        P("pipe", None, "expert", None),
        P("pipe", None, "expert", None),
    )
    out_specs = (P("pipe", None, "expert", None), P("pipe", None, "expert", None))
    return jax.shard_map(
        on_device, mesh=mesh, in_specs=in_specs, out_specs=out_specs, check_vma=False
    )
```

```python
import functools

import jax
import jax.numpy as jnp
from jax import lax
from jax.experimental import pallas as pl
from jax.experimental.pallas import tpu as pltpu
from jax.sharding import PartitionSpec as P

BLOCKS = 2
HIDS = 256


def spans(size, step):
    return [slice(at, at + step) for at in range(0, size, step)]


def expert_kernel(count, *refs):
    blocks, refs = refs[:count], refs[count:]
    pick_ref, put_ref, weight_ref, gain_ref, gate_hbm, up_hbm, down_hbm = refs[:7]
    outs, refs = refs[7 : 7 + count], refs[7 + count :]
    rows_ref, picked, hidden, gate_ref, up_ref, down_ref, sems = refs
    tokens = blocks[0].shape[0]
    width, hid = gate_ref.shape
    wides, hids = spans(width, width // BLOCKS), spans(hid, HIDS)

    def streams(at, step):
        return [
            pltpu.make_async_copy(source.at[:, at], target.at[:, at], sems.at[2 * step + i])
            for i, (source, target) in enumerate(((gate_hbm, gate_ref), (up_hbm, up_ref)))
        ]

    for step, at in enumerate(hids):
        for copy in streams(at, step):
            copy.start()
    lasts = [
        pltpu.make_async_copy(down_hbm.at[:, at], down_ref.at[:, at], sems.at[2 * len(hids) + i])
        for i, at in enumerate(wides)
    ]
    for copy in lasts:
        copy.start()

    for i, ref in enumerate(blocks):
        rows_ref[i * tokens : (i + 1) * tokens] = ref[...]
    total = 0.0
    for at in wides:
        block = jnp.dot(pick_ref[...], rows_ref[:, at], preferred_element_type=jnp.float32)
        picked[:, at] = block.astype(jnp.bfloat16)
        total += jnp.sum(block * block, axis=1, keepdims=True)
    scale = lax.rsqrt(total / width + 1e-06)
    for at in wides:
        block = picked[:, at].astype(jnp.float32) * scale * gain_ref[:, at]
        picked[:, at] = block.astype(jnp.bfloat16)

    def project(step, carry):
        at = pl.ds(pl.multiple_of(step * HIDS, HIDS), HIDS)
        for copy in streams(at, step):
            copy.wait()
        first = jnp.dot(picked[...], gate_ref[:, at], preferred_element_type=jnp.float32)
        second = jnp.dot(picked[...], up_ref[:, at], preferred_element_type=jnp.float32)
        hidden[:, at] = (first / (1.0 + jnp.exp(-first)) * second).astype(jnp.bfloat16)
        return carry

    lax.fori_loop(0, len(hids), project, 0)
    for at, copy in zip(wides, lasts):
        copy.wait()
        block = jnp.dot(hidden[...], down_ref[:, at], preferred_element_type=jnp.float32)
        block = jnp.dot(put_ref[...], block.astype(jnp.bfloat16), preferred_element_type=jnp.float32)
        block = (block * weight_ref[...]).astype(jnp.bfloat16)
        for i, ref in enumerate(outs):
            ref[:, at] = block[i * tokens : (i + 1) * tokens]


def expert_call(blocks, pick, put, weight, gain, gate_cols, up_cols, down_rows):
    count, (tokens, width) = len(blocks), blocks[0].shape
    slots, hid = pick.shape[0], gate_cols.shape[1]
    whole = pl.BlockSpec(memory_space=pltpu.VMEM)
    return pl.pallas_call(
        functools.partial(expert_kernel, count),
        out_shape=[jax.ShapeDtypeStruct((tokens, width), jnp.bfloat16)] * count,
        in_specs=[whole] * (count + 4) + [pl.BlockSpec(memory_space=pltpu.HBM)] * 3,
        out_specs=[whole] * count,
        scratch_shapes=[
            pltpu.VMEM((count * tokens, width), jnp.bfloat16),
            pltpu.VMEM((slots, width), jnp.bfloat16),
            pltpu.VMEM((slots, hid), jnp.bfloat16),
            pltpu.VMEM((width, hid), jnp.bfloat16),
            pltpu.VMEM((width, hid), jnp.bfloat16),
            pltpu.VMEM((hid, width), jnp.bfloat16),
            pltpu.SemaphoreType.DMA((2 * (hid // HIDS) + BLOCKS,)),
        ],
        compiler_params=pltpu.CompilerParams(vmem_limit_bytes=(24 + count * tokens // 64) * 2**20),
        cost_estimate=pl.CostEstimate(
            flops=6 * slots * width * hid, bytes_accessed=6 * width * hid, transcendentals=slots * hid
        ),
    )(*blocks, pick, put, weight, gain, *(
        pltpu.with_memory_space_constraint(w, pltpu.HBM) for w in (gate_cols, up_cols, down_rows)
    ))


def after(values, earlier):
    return lax.optimization_barrier((values, earlier))


def on_device(
    tokens_up, tokens_down, norm_gain, w_gate, w_up, w_down, route_up, route_down, gate_up, gate_down
):
    plane, me = lax.axis_index("pipe"), lax.axis_index("expert")
    planes, experts = lax.axis_size("pipe"), lax.axis_size("expert")
    micros, tokens, width = tokens_up.shape
    top = route_up.shape[3]
    capacity = min(tokens, 2 * tokens * top // experts)
    low = plane < planes // 2
    layer = (norm_gain, w_gate[0], w_up[0], w_down[0])
    masks = list(range(0, experts, 2)) + list(range(1, experts, 2))
    half = experts // 2

    def exchange(block, mask):
        return lax.ppermute(block, "expert", [(i, i ^ mask) for i in range(experts)])

    def on_chip(outs):
        total = [
            a.astype(jnp.float32) + exchange(b, 1).astype(jnp.float32)
            for a, b in zip(outs[:half], outs[half:])
        ]
        return total[:1] + [part.astype(jnp.bfloat16) for part in total[1:]]

    def send_back(sums):
        return sums[:1] + [exchange(sums[j], masks[j]) for j in range(1, half)]

    def ordered(up, down):
        return [jnp.where(low, up, down), jnp.where(low, down, up)]

    tables = jnp.stack(
        [
            jnp.stack(ordered(route_up[0].astype(jnp.float32), route_down[0].astype(jnp.float32))),
            jnp.stack(ordered(gate_up[0], gate_down[0])),
        ]
    )
    pair = jnp.stack([tables, exchange(tables, 1)])
    tables = jnp.stack([pair] + [exchange(pair, mask) for mask in masks[1:half]], axis=1)
    tables = tables.reshape(experts, *pair.shape[1:])
    hits = (tables[:, 0] == me.astype(jnp.float32)).astype(jnp.float32)
    weights = jnp.sum(hits * tables[:, 1], axis=-1)
    hits = jnp.sum(hits, axis=-1)
    before = (jnp.arange(tokens)[:, None] < jnp.arange(tokens)[None, :]).astype(jnp.float32)
    places = jnp.einsum("dsmt,tu->dsmu", hits, before)
    places += capacity * jnp.arange(experts, dtype=jnp.float32)[:, None, None, None]
    places = jnp.where(hits > 0, places, -1.0)
    places = places.transpose(1, 2, 0, 3).reshape(2, micros, experts * tokens)
    weights = weights.transpose(1, 2, 0, 3).reshape(2, micros, experts * tokens, 1)
    slots = jnp.arange(experts * capacity, dtype=jnp.float32)
    pick = (places[:, :, None, :] == slots[:, None]).astype(jnp.bfloat16)
    put = (places[:, :, :, None] == slots).astype(jnp.bfloat16)

    entering = [jnp.where(low, tokens_up[m], tokens_down[m]) for m in range(micros)]
    results = []
    for tick in range(planes):
        stream = 0 if tick < planes // 2 else 1
        near, sums, back = [], [], []
        for m in range(micros):
            own = entering[m]
            if m > 0:
                own, near[m - 1] = after(own, near[m - 1])
            arrived = [exchange(own, mask) for mask in masks[1:half]]
            if m > 0:
                arrived, outs = after(arrived, outs)
                sums.append(on_chip(outs))
                arrived, sums[m - 1] = after(arrived, sums[m - 1])
                back.append(send_back(sums[m - 1]))
            near.append([entering[m]] + arrived)
            far = [exchange(block, 1) for block in near[m]]
            outs = expert_call(
                near[m] + far, pick[stream, m], put[stream, m], weights[stream, m], *layer
            )
            if m > 0:
                back[m - 1], outs = after(back[m - 1], outs)
        sums.append(on_chip(outs))
        back.append(send_back(sums[-1]))
        leaving = []
        for m in range(micros):
            total = entering[m].astype(jnp.float32)
            for part in back[m]:
                total += part.astype(jnp.float32)
            leaving.append(total.astype(jnp.bfloat16))
        results.append(leaving)
        if tick + 1 < planes:
            ups = [(p, p + 1) for p in range(tick % 2, planes - 1, 2)]
            pairs = ups + [(b, a) for a, b in ups]
            entering = [lax.ppermute(block, "pipe", pairs) for block in leaving]

    first = jnp.minimum(plane, planes - 1 - plane)
    acts = []
    for ticks, at in (
        (range(planes // 2), first),
        (range(planes // 2, planes), planes - 1 - first),
    ):
        chosen = jnp.stack(results[ticks[0]])
        for tick in ticks[1:]:
            chosen = jnp.where(at == tick, jnp.stack(results[tick]), chosen)
        acts.append(chosen)
    return (jnp.where(low, acts[0], acts[1])[None], jnp.where(low, acts[1], acts[0])[None])


def solution(mesh):
    in_specs = (
        P(None, "expert", None),
        P(None, "expert", None),
        P("pipe", None),
        P("pipe", None, "expert"),
        P("pipe", None, "expert"),
        P("pipe", "expert", None),
        P("pipe", None, "expert", None),
        P("pipe", None, "expert", None),
        P("pipe", None, "expert", None),
        P("pipe", None, "expert", None),
    )
    out_specs = (P("pipe", None, "expert", None), P("pipe", None, "expert", None))
    return jax.shard_map(
        on_device, mesh=mesh, in_specs=in_specs, out_specs=out_specs, check_vma=False
    )
```

```python
import functools

import jax
import jax.numpy as jnp
from jax import lax
from jax.experimental import pallas as pl
from jax.experimental.pallas import tpu as pltpu
from jax.sharding import PartitionSpec as P

BLOCKS = 2
HIDS = 256


def spans(size, step):
    return [slice(at, at + step) for at in range(0, size, step)]


def expert_kernel(count, *refs):
    blocks, refs = refs[:count], refs[count:]
    pick_ref, put_ref, weight_ref, gain_ref, gate_hbm, up_hbm, down_hbm = refs[:7]
    outs, refs = refs[7 : 7 + count], refs[7 + count :]
    rows_ref, picked, hidden, gate_ref, up_ref, down_ref, sems = refs
    tokens = blocks[0].shape[0]
    width, hid = gate_ref.shape
    wides, hids = spans(width, width // BLOCKS), spans(hid, HIDS)

    def streams(at, step):
        return [
            pltpu.make_async_copy(source.at[:, at], target.at[:, at], sems.at[2 * step + i])
            for i, (source, target) in enumerate(((gate_hbm, gate_ref), (up_hbm, up_ref)))
        ]

    for step, at in enumerate(hids):
        for copy in streams(at, step):
            copy.start()
    lasts = [
        pltpu.make_async_copy(down_hbm.at[:, at], down_ref.at[:, at], sems.at[2 * len(hids) + i])
        for i, at in enumerate(wides)
    ]
    for copy in lasts:
        copy.start()

    for i, ref in enumerate(blocks):
        rows_ref[i * tokens : (i + 1) * tokens] = ref[...]
    total = 0.0
    for at in wides:
        block = jnp.dot(pick_ref[...], rows_ref[:, at], preferred_element_type=jnp.float32)
        picked[:, at] = block.astype(jnp.bfloat16)
        total += jnp.sum(block * block, axis=1, keepdims=True)
    scale = lax.rsqrt(total / width + 1e-06)
    for at in wides:
        block = picked[:, at].astype(jnp.float32) * scale * gain_ref[:, at]
        picked[:, at] = block.astype(jnp.bfloat16)

    def project(step, carry):
        at = pl.ds(pl.multiple_of(step * HIDS, HIDS), HIDS)
        for copy in streams(at, step):
            copy.wait()
        first = jnp.dot(picked[...], gate_ref[:, at], preferred_element_type=jnp.float32)
        second = jnp.dot(picked[...], up_ref[:, at], preferred_element_type=jnp.float32)
        hidden[:, at] = (first / (1.0 + jnp.exp(-first)) * second).astype(jnp.bfloat16)
        return carry

    lax.fori_loop(0, len(hids), project, 0)
    for at, copy in zip(wides, lasts):
        copy.wait()
        block = jnp.dot(hidden[...], down_ref[:, at], preferred_element_type=jnp.float32)
        block = jnp.dot(put_ref[...], block.astype(jnp.bfloat16), preferred_element_type=jnp.float32)
        block = (block * weight_ref[...]).astype(jnp.bfloat16)
        for i, ref in enumerate(outs):
            ref[:, at] = block[i * tokens : (i + 1) * tokens]


def expert_call(blocks, pick, put, weight, gain, gate_cols, up_cols, down_rows):
    count, (tokens, width) = len(blocks), blocks[0].shape
    slots, hid = pick.shape[0], gate_cols.shape[1]
    whole = pl.BlockSpec(memory_space=pltpu.VMEM)
    return pl.pallas_call(
        functools.partial(expert_kernel, count),
        out_shape=[jax.ShapeDtypeStruct((tokens, width), jnp.bfloat16)] * count,
        in_specs=[whole] * (count + 4) + [pl.BlockSpec(memory_space=pltpu.HBM)] * 3,
        out_specs=[whole] * count,
        scratch_shapes=[
            pltpu.VMEM((count * tokens, width), jnp.bfloat16),
            pltpu.VMEM((slots, width), jnp.bfloat16),
            pltpu.VMEM((slots, hid), jnp.bfloat16),
            pltpu.VMEM((width, hid), jnp.bfloat16),
            pltpu.VMEM((width, hid), jnp.bfloat16),
            pltpu.VMEM((hid, width), jnp.bfloat16),
            pltpu.SemaphoreType.DMA((2 * (hid // HIDS) + BLOCKS,)),
        ],
        compiler_params=pltpu.CompilerParams(vmem_limit_bytes=(20 + count * tokens // 64) * 2**20),
        cost_estimate=pl.CostEstimate(
            flops=6 * slots * width * hid, bytes_accessed=6 * width * hid, transcendentals=slots * hid
        ),
    )(*blocks, pick, put, weight, gain, *(
        pltpu.with_memory_space_constraint(w, pltpu.HBM) for w in (gate_cols, up_cols, down_rows)
    ))


def after(values, earlier):
    return lax.optimization_barrier((values, earlier))


def on_device(
    tokens_up, tokens_down, norm_gain, w_gate, w_up, w_down, route_up, route_down, gate_up, gate_down
):
    plane, me = lax.axis_index("pipe"), lax.axis_index("expert")
    planes, experts = lax.axis_size("pipe"), lax.axis_size("expert")
    micros, tokens, width = tokens_up.shape
    top = route_up.shape[3]
    capacity = min(tokens, 2 * tokens * top // experts)
    low = plane < planes // 2
    layer = (norm_gain, w_gate[0], w_up[0], w_down[0])
    masks = list(range(0, experts, 2)) + list(range(1, experts, 2))
    half = experts // 2

    def exchange(block, mask):
        return lax.ppermute(block, "expert", [(i, i ^ mask) for i in range(experts)])

    def on_chip(outs):
        mine, other = outs[1:half] + outs[:1], outs[half + 1 :] + outs[half : half + 1]
        total = [
            a.astype(jnp.float32) + exchange(b, 1).astype(jnp.float32)
            for a, b in zip(mine, other)
        ]
        total = total[-1:] + total[:-1]
        return total[:1] + [part.astype(jnp.bfloat16) for part in total[1:]]

    def send_back(sums):
        return sums[:1] + [exchange(sums[j], masks[j]) for j in range(1, half)]

    def ordered(up, down):
        return [jnp.where(low, up, down), jnp.where(low, down, up)]

    tables = jnp.stack(
        [
            jnp.stack(ordered(route_up[0].astype(jnp.float32), route_down[0].astype(jnp.float32))),
            jnp.stack(ordered(gate_up[0], gate_down[0])),
        ]
    )
    pair = jnp.stack([tables, exchange(tables, 1)])
    tables = jnp.stack([pair] + [exchange(pair, mask) for mask in masks[1:half]], axis=1)
    tables = tables.reshape(experts, *pair.shape[1:])
    hits = (tables[:, 0] == me.astype(jnp.float32)).astype(jnp.float32)
    weights = jnp.sum(hits * tables[:, 1], axis=-1)
    hits = jnp.sum(hits, axis=-1)
    before = (jnp.arange(tokens)[:, None] < jnp.arange(tokens)[None, :]).astype(jnp.float32)
    places = jnp.einsum("dsmt,tu->dsmu", hits, before)
    places += capacity * jnp.arange(experts, dtype=jnp.float32)[:, None, None, None]
    places = jnp.where(hits > 0, places, -1.0)
    places = places.transpose(1, 2, 0, 3).reshape(2, micros, experts * tokens)
    weights = weights.transpose(1, 2, 0, 3).reshape(2, micros, experts * tokens, 1)
    slots = jnp.arange(experts * capacity, dtype=jnp.float32)
    pick = (places[:, :, None, :] == slots[:, None]).astype(jnp.bfloat16)
    put = (places[:, :, :, None] == slots).astype(jnp.bfloat16)

    entering = [jnp.where(low, tokens_up[m], tokens_down[m]) for m in range(micros)]
    results = []
    for tick in range(planes):
        stream = 0 if tick < planes // 2 else 1
        near, sums, back, leaving = [], [], [], []
        for m in range(micros):
            own = entering[m]
            if m > 0:
                own, near[m - 1] = after(own, near[m - 1])
            arrived = [exchange(own, mask) for mask in masks[1:half]]
            if m > 0:
                arrived, outs = after(arrived, outs)
                sums.append(on_chip(outs))
                arrived, sums[m - 1] = after(arrived, sums[m - 1])
                back.append(send_back(sums[m - 1]))
            near.append([entering[m]] + arrived)
            far = [exchange(block, 1) for block in near[m]]
            outs = expert_call(
                near[m] + far, pick[stream, m], put[stream, m], weights[stream, m], *layer
            )
            if m > 0:
                back[m - 1], outs = after(back[m - 1], outs)
                total = entering[m - 1].astype(jnp.float32)
                for part in back[m - 1]:
                    total += part.astype(jnp.float32)
                done, outs = after(total.astype(jnp.bfloat16), outs)
                leaving.append(done)
        sums.append(on_chip(outs))
        back.append(send_back(sums[-1]))
        total = entering[-1].astype(jnp.float32)
        for part in back[-1]:
            total += part.astype(jnp.float32)
        leaving.append(total.astype(jnp.bfloat16))
        results.append(leaving)
        if tick + 1 < planes:
            ups = [(p, p + 1) for p in range(tick % 2, planes - 1, 2)]
            pairs = ups + [(b, a) for a, b in ups]
            entering = [lax.ppermute(block, "pipe", pairs) for block in leaving]

    first = jnp.minimum(plane, planes - 1 - plane)
    acts = []
    for ticks, at in (
        (range(planes // 2), first),
        (range(planes // 2, planes), planes - 1 - first),
    ):
        chosen = jnp.stack(results[ticks[0]])
        for tick in ticks[1:]:
            chosen = jnp.where(at == tick, jnp.stack(results[tick]), chosen)
        acts.append(chosen)
    return (jnp.where(low, acts[0], acts[1])[None], jnp.where(low, acts[1], acts[0])[None])


def solution(mesh):
    in_specs = (
        P(None, "expert", None),
        P(None, "expert", None),
        P("pipe", None),
        P("pipe", None, "expert"),
        P("pipe", None, "expert"),
        P("pipe", "expert", None),
        P("pipe", None, "expert", None),
        P("pipe", None, "expert", None),
        P("pipe", None, "expert", None),
        P("pipe", None, "expert", None),
    )
    out_specs = (P("pipe", None, "expert", None), P("pipe", None, "expert", None))
    return jax.shard_map(
        on_device, mesh=mesh, in_specs=in_specs, out_specs=out_specs, check_vma=False
    )
```

```python
import functools

import jax
import jax.numpy as jnp
from jax import lax
from jax.experimental import pallas as pl
from jax.experimental.pallas import tpu as pltpu
from jax.sharding import PartitionSpec as P

BLOCKS = 2
HIDS = 256


def spans(size, step):
    return [slice(at, at + step) for at in range(0, size, step)]


def expert_kernel(count, *refs):
    blocks, refs = refs[:count], refs[count:]
    pick_ref, put_ref, weight_ref, gain_ref, gate_hbm, up_hbm, down_hbm = refs[:7]
    outs, refs = refs[7 : 7 + count], refs[7 + count :]
    rows_ref, picked, hidden, gate_ref, up_ref, down_ref, sems = refs
    tokens = blocks[0].shape[0]
    width, hid = gate_ref.shape
    wides, hids = spans(width, width // BLOCKS), spans(hid, HIDS)

    def streams(at, step):
        return [
            pltpu.make_async_copy(source.at[:, at], target.at[:, at], sems.at[2 * step + i])
            for i, (source, target) in enumerate(((gate_hbm, gate_ref), (up_hbm, up_ref)))
        ]

    for step, at in enumerate(hids):
        for copy in streams(at, step):
            copy.start()
    lasts = [
        pltpu.make_async_copy(down_hbm.at[:, at], down_ref.at[:, at], sems.at[2 * len(hids) + i])
        for i, at in enumerate(wides)
    ]
    for copy in lasts:
        copy.start()

    for i, ref in enumerate(blocks):
        rows_ref[i * tokens : (i + 1) * tokens] = ref[...]
    total = 0.0
    for at in wides:
        block = jnp.dot(pick_ref[...], rows_ref[:, at], preferred_element_type=jnp.float32)
        picked[:, at] = block.astype(jnp.bfloat16)
        total += jnp.sum(block * block, axis=1, keepdims=True)
    scale = lax.rsqrt(total / width + 1e-06)
    for at in wides:
        block = picked[:, at].astype(jnp.float32) * scale * gain_ref[:, at]
        picked[:, at] = block.astype(jnp.bfloat16)

    def project(step, carry):
        at = pl.ds(pl.multiple_of(step * HIDS, HIDS), HIDS)
        for copy in streams(at, step):
            copy.wait()
        first = jnp.dot(picked[...], gate_ref[:, at], preferred_element_type=jnp.float32)
        second = jnp.dot(picked[...], up_ref[:, at], preferred_element_type=jnp.float32)
        hidden[:, at] = (first / (1.0 + jnp.exp(-first)) * second).astype(jnp.bfloat16)
        return carry

    lax.fori_loop(0, len(hids), project, 0)
    for at, copy in zip(wides, lasts):
        copy.wait()
        block = jnp.dot(hidden[...], down_ref[:, at], preferred_element_type=jnp.float32)
        block = jnp.dot(put_ref[...], block.astype(jnp.bfloat16), preferred_element_type=jnp.float32)
        block = (block * weight_ref[...]).astype(jnp.bfloat16)
        for i, ref in enumerate(outs):
            ref[:, at] = block[i * tokens : (i + 1) * tokens]


def expert_call(blocks, pick, put, weight, gain, gate_cols, up_cols, down_rows):
    count, (tokens, width) = len(blocks), blocks[0].shape
    slots, hid = pick.shape[0], gate_cols.shape[1]
    whole = pl.BlockSpec(memory_space=pltpu.VMEM)
    return pl.pallas_call(
        functools.partial(expert_kernel, count),
        out_shape=[jax.ShapeDtypeStruct((tokens, width), jnp.bfloat16)] * count,
        in_specs=[whole] * (count + 4) + [pl.BlockSpec(memory_space=pltpu.HBM)] * 3,
        out_specs=[whole] * count,
        scratch_shapes=[
            pltpu.VMEM((count * tokens, width), jnp.bfloat16),
            pltpu.VMEM((slots, width), jnp.bfloat16),
            pltpu.VMEM((slots, hid), jnp.bfloat16),
            pltpu.VMEM((width, hid), jnp.bfloat16),
            pltpu.VMEM((width, hid), jnp.bfloat16),
            pltpu.VMEM((hid, width), jnp.bfloat16),
            pltpu.SemaphoreType.DMA((2 * (hid // HIDS) + BLOCKS,)),
        ],
        compiler_params=pltpu.CompilerParams(vmem_limit_bytes=(20 + count * tokens // 64) * 2**20),
        cost_estimate=pl.CostEstimate(
            flops=6 * slots * width * hid, bytes_accessed=6 * width * hid, transcendentals=slots * hid
        ),
    )(*blocks, pick, put, weight, gain, *(
        pltpu.with_memory_space_constraint(w, pltpu.HBM) for w in (gate_cols, up_cols, down_rows)
    ))


def after(values, earlier):
    return lax.optimization_barrier((values, earlier))


def on_device(
    tokens_up, tokens_down, norm_gain, w_gate, w_up, w_down, route_up, route_down, gate_up, gate_down
):
    plane, me = lax.axis_index("pipe"), lax.axis_index("expert")
    planes, experts = lax.axis_size("pipe"), lax.axis_size("expert")
    micros, tokens, width = tokens_up.shape
    top = route_up.shape[3]
    capacity = min(tokens, 2 * tokens * top // experts)
    low = plane < planes // 2
    layer = (norm_gain, w_gate[0], w_up[0], w_down[0])
    masks = list(range(0, experts, 2)) + list(range(1, experts, 2))
    half = experts // 2

    def exchange(block, mask):
        return lax.ppermute(block, "expert", [(i, i ^ mask) for i in range(experts)])

    def on_chip(outs):
        mine, other = outs[1:half] + outs[:1], outs[half + 1 :] + outs[half : half + 1]
        total = [
            a.astype(jnp.float32) + exchange(b, 1).astype(jnp.float32)
            for a, b in zip(mine, other)
        ]
        total = total[-1:] + total[:-1]
        return total[:1] + [part.astype(jnp.bfloat16) for part in total[1:]]

    def send_back(sums):
        return sums[:1] + [exchange(sums[j], masks[j]) for j in range(1, half)]

    def ordered(up, down):
        return [jnp.where(low, up, down), jnp.where(low, down, up)]

    tables = jnp.stack(
        [
            jnp.stack(ordered(route_up[0].astype(jnp.float32), route_down[0].astype(jnp.float32))),
            jnp.stack(ordered(gate_up[0], gate_down[0])),
        ]
    )
    pair = jnp.stack([tables, exchange(tables, 1)])
    tables = jnp.stack([pair] + [exchange(pair, mask) for mask in masks[1:half]], axis=1)
    tables = tables.reshape(experts, *pair.shape[1:])
    hits = (tables[:, 0] == me.astype(jnp.float32)).astype(jnp.float32)
    weights = jnp.sum(hits * tables[:, 1], axis=-1)
    hits = jnp.sum(hits, axis=-1)
    before = (jnp.arange(tokens)[:, None] < jnp.arange(tokens)[None, :]).astype(jnp.float32)
    places = jnp.einsum("dsmt,tu->dsmu", hits, before)
    places += capacity * jnp.arange(experts, dtype=jnp.float32)[:, None, None, None]
    places = jnp.where(hits > 0, places, -1.0)
    places = places.transpose(1, 2, 0, 3).reshape(2, micros, experts * tokens)
    weights = weights.transpose(1, 2, 0, 3).reshape(2, micros, experts * tokens, 1)
    slots = jnp.arange(experts * capacity, dtype=jnp.float32)
    pick = (places[:, :, None, :] == slots[:, None]).astype(jnp.bfloat16)
    put = (places[:, :, :, None] == slots).astype(jnp.bfloat16)

    entering = [jnp.where(low, tokens_up[m], tokens_down[m]) for m in range(micros)]
    results = []
    for tick in range(planes):
        stream = 0 if tick < planes // 2 else 1
        near, sums, back, leaving = [], [], [], []
        for m in range(micros):
            own = entering[m]
            if m > 0:
                own, near[m - 1] = after(own, near[m - 1])
            far_own = exchange(entering[m], 1)
            arrived = [exchange(own, mask) for mask in masks[1:half]]
            if m > 0:
                (arrived, far_own), outs = after((arrived, far_own), outs)
                sums.append(on_chip(outs))
                arrived, sums[m - 1] = after(arrived, sums[m - 1])
                back.append(send_back(sums[m - 1]))
            near.append([entering[m]] + arrived)
            far = [far_own] + [exchange(block, 1) for block in near[m][1:]]
            outs = expert_call(
                near[m] + far, pick[stream, m], put[stream, m], weights[stream, m], *layer
            )
            if m > 0:
                back[m - 1], outs = after(back[m - 1], outs)
                total = entering[m - 1].astype(jnp.float32)
                for part in back[m - 1]:
                    total += part.astype(jnp.float32)
                done, outs = after(total.astype(jnp.bfloat16), outs)
                leaving.append(done)
        sums.append(on_chip(outs))
        back.append(send_back(sums[-1]))
        total = entering[-1].astype(jnp.float32)
        for part in back[-1]:
            total += part.astype(jnp.float32)
        leaving.append(total.astype(jnp.bfloat16))
        results.append(leaving)
        if tick + 1 < planes:
            ups = [(p, p + 1) for p in range(tick % 2, planes - 1, 2)]
            pairs = ups + [(b, a) for a, b in ups]
            entering = [lax.ppermute(block, "pipe", pairs) for block in leaving]

    first = jnp.minimum(plane, planes - 1 - plane)
    acts = []
    for ticks, at in (
        (range(planes // 2), first),
        (range(planes // 2, planes), planes - 1 - first),
    ):
        chosen = jnp.stack(results[ticks[0]])
        for tick in ticks[1:]:
            chosen = jnp.where(at == tick, jnp.stack(results[tick]), chosen)
        acts.append(chosen)
    return (jnp.where(low, acts[0], acts[1])[None], jnp.where(low, acts[1], acts[0])[None])


def solution(mesh):
    in_specs = (
        P(None, "expert", None),
        P(None, "expert", None),
        P("pipe", None),
        P("pipe", None, "expert"),
        P("pipe", None, "expert"),
        P("pipe", "expert", None),
        P("pipe", None, "expert", None),
        P("pipe", None, "expert", None),
        P("pipe", None, "expert", None),
        P("pipe", None, "expert", None),
    )
    out_specs = (P("pipe", None, "expert", None), P("pipe", None, "expert", None))
    return jax.shard_map(
        on_device, mesh=mesh, in_specs=in_specs, out_specs=out_specs, check_vma=False
    )
```
